32 devices in a mesh: gx: 2 (over y), gy: 4 (over x, core), gz: 4 (over z).
Axes of the slice: x: 2, y: 2, z: 4, core: 2. Of those that a mesh axis runs over, the one named last changes fastest.
Arguments:
- features: bfloat16 [8, 32, 2048], P('gx', 'gy', 'gz'), may hold values from -6 to 6
- upstream: bfloat16 [8, 32, 2048], P('gx', 'gy', 'gz'), may hold values from -6 to 6
- params: float32 [718848], P(('gx', 'gy', 'gz')), may hold values from -1 to 1
- first_moment: float32 [718848], P(('gx', 'gy', 'gz')), may hold values from -1 to 1
- second_moment: float32 [718848], P(('gx', 'gy', 'gz')), may hold values from 0.0005 to 0.005
Outputs:
- refined: bfloat16 [8, 32, 2048], P('gx', 'gy', 'gz')
- new_params: float32 [718848], P(('gx', 'gy', 'gz'))
- new_first: float32 [718848], P(('gx', 'gy', 'gz'))
- new_second: float32 [718848], P(('gx', 'gy', 'gz'))
The draws below stay inside these ranges and needn't reach their ends.
All inputs are finite; a program needn't handle non-finite values.
Results may differ from the reference program's by a relative error of at most 0.01.
The reference program's roundings to bfloat16 on the way count: a program that leaves them out, or rounds other values in their place, can miss the bound.
Values may be sent and summed in bfloat16 or wider, within the bound.
A program may use at most 128 MiB of HBM per device.

```python
import math
import jax
import jax.numpy as jnp
from jax import lax

C = 64
G = 32
STEP = 3
NX = 8
NY = 32
NZ = 32
PARAMS = 718848


def draw_params(key, part):
    shapes = [(G, C + layer * G) for layer in range(4)] + [(C, C + 4 * G)]
    segments = []
    for layer in range(5):
        outputs, inputs = shapes[layer]
        sub_key = jax.random.fold_in(key, 11 + layer)
        spread = (27.0 * inputs) ** (-0.5)
        values = jnp.clip(jax.random.normal(sub_key, (27 * outputs * inputs,), jnp.float32), -3.0, 3.0) * spread
        segments.append(values)
    return jnp.concatenate(segments)


def level_of(stream_key, extent, cuts, smallest, largest):
    loudness = 1.0
    for axis_at, shards_of in cuts:
        heights = jax.random.uniform(jax.random.fold_in(jax.random.fold_in(stream_key, 6), axis_at), (shards_of,), jnp.float32, smallest / len(cuts), largest / len(cuts))
        loudness = loudness * jnp.repeat(jnp.exp(heights), extent[axis_at] // shards_of).reshape((-1,) + (1,) * (len(extent) - 1 - axis_at))
    return loudness


def centred(rng, shape, deviation, most, shards=(), dtype=jnp.bfloat16):
    loudness = level_of(rng, shape, shards, -0.22, 0.18) if shards else 1.0
    values = jax.random.normal(rng, shape, jnp.float32) * deviation * loudness
    return jnp.minimum(jnp.maximum(values, -most), most).astype(dtype)


def setup_inputs(seed: int = 0) -> dict:
    keys = jax.random.split(jax.random.key(seed), 6)
    return {
        "features": centred(keys[0], (NX, NY, NZ * C), 1.0, 6.0, ((0, 2), (1, 4), (2, 4))),
        "upstream": centred(keys[1], (NX, NY, NZ * C), 1.0, 6.0, ((0, 2), (1, 4), (2, 4))),
        "params": draw_params(jax.random.fold_in(keys[5], 71), 0),
        "first_moment": centred(keys[3], (PARAMS,), 0.2, 1.0, ((0, 32),), jnp.float32),
        "second_moment": jnp.clip(jnp.exp(math.log(0.005) - 2.30258502 * jax.random.uniform(keys[4], (PARAMS,), jnp.float32) ** level_of(keys[4], (PARAMS,), ((0, 32),), -0.2, 0.2)), 0.0005, 0.005),
    }


LEAK_SLOPE = 0.2
RESIDUAL_SCALE = 0.2
BETA_ONE = 0.9
BETA_TWO = 0.999
LEARN_RATE = 0.001
ADAM_EPS = 1e-08
NORM_EPS = 1e-06

def layer_shapes():
    return [(G, C + layer * G) for layer in range(4)] + [(C, C + 4 * G)]

def split_kernels(flat_weights):
    kernel_list = []
    offset = 0
    for outputs, inputs in layer_shapes():
        length = 27 * outputs * inputs
        kernel_list.append(flat_weights[offset:offset + length].reshape(27, outputs, inputs))
        offset = offset + length
    return kernel_list

def correlate(values_in, kernel):
    weight = kernel.astype(jnp.float32).reshape(3, 3, 3, kernel.shape[1], kernel.shape[2]).transpose(3, 4, 0, 1, 2)
    result = lax.conv_general_dilated(values_in.astype(jnp.float32)[None], weight, (1, 1, 1), [(1, 1), (1, 1), (1, 1)], dimension_numbers=('NCDHW', 'OIDHW', 'NCDHW'), precision=lax.Precision.HIGHEST)
    return result[0]

def channels_first(packed):
    return packed.reshape(packed.shape[0], packed.shape[1], -1, C).transpose(3, 0, 1, 2)

def reference(features, upstream, params, first_moment, second_moment):
    field = channels_first(features)
    dout = channels_first(upstream)
    kernel_list = split_kernels(params.astype(jnp.bfloat16))
    pieces = [field]
    slopes = []
    for layer in range(4):
        before = correlate(jnp.concatenate(pieces, 0), kernel_list[layer])
        slope_now = jnp.where(before > 0, 1.0, LEAK_SLOPE).astype(jnp.float32)
        slopes.append(slope_now)
        pieces.append((before * slope_now).astype(jnp.bfloat16))
    inputs_list = [jnp.concatenate(pieces[:layer + 1], 0) for layer in range(5)]
    last = correlate(inputs_list[4], kernel_list[4])
    refined_first = (field.astype(jnp.float32) + RESIDUAL_SCALE * last).astype(jnp.bfloat16)
    refined = refined_first.transpose(1, 2, 3, 0).reshape(features.shape)
    signals = [None] * 5
    signals[4] = (RESIDUAL_SCALE * dout.astype(jnp.float32)).astype(jnp.bfloat16)
    backward = [jnp.zeros((G,) + field.shape[1:], jnp.float32) for layer in range(4)]
    for layer in range(4, 0, -1):
        kernel_now = kernel_list[layer]

        def convolve(values_in):
            return correlate(values_in, kernel_now)
        unused, pullback = jax.vjp(convolve, inputs_list[layer].astype(jnp.float32))
        spread = pullback(signals[layer].astype(jnp.float32))[0]
        for target in range(layer):
            backward[target] = backward[target] + spread[C + target * G:C + (target + 1) * G]
        signals[layer - 1] = (backward[layer - 1] * slopes[layer - 1]).astype(jnp.bfloat16)
    grads = []
    for layer in range(5):
        input_now = inputs_list[layer]

        def convolve_kernel(kernel):
            return correlate(input_now, kernel)
        unused, pullback = jax.vjp(convolve_kernel, kernel_list[layer].astype(jnp.float32))
        grads.append(pullback(signals[layer].astype(jnp.float32))[0].reshape(-1))
    gradient = jnp.concatenate(grads)
    norm_sq = jnp.sum(gradient * gradient)
    factor = jnp.minimum(1.0, jnp.sqrt(PARAMS / (norm_sq + NORM_EPS)))
    clipped = gradient * factor
    new_first = BETA_ONE * first_moment + (1.0 - BETA_ONE) * clipped
    new_second = BETA_TWO * second_moment + (1.0 - BETA_TWO) * clipped * clipped
    first_hat = new_first / (1.0 - BETA_ONE ** STEP)
    second_hat = new_second / (1.0 - BETA_TWO ** STEP)
    new_params = params - LEARN_RATE * first_hat / (jnp.sqrt(second_hat) + ADAM_EPS)
    return (refined, new_params, new_first, new_second)
```

```python
import functools

import jax
import jax.numpy as jnp
from jax import lax
from jax.experimental import pallas as pl
from jax.experimental.pallas import tpu as pltpu
from jax.sharding import PartitionSpec as P

MESH = pl.DeviceIdType.MESH

C = 64
G = 32
STEP = 3


LEAK_SLOPE = 0.2
RESIDUAL_SCALE = 0.2
BETA_ONE = 0.9
BETA_TWO = 0.999
LEARN_RATE = 0.001
ADAM_EPS = 1e-08
NORM_EPS = 1e-06


def extended(cells, sides, width):
    for axis, dim in sides:
        count = lax.axis_size(axis)
        ends = count - 1
        head = lax.slice_in_dim(cells, 0, width, axis=dim)
        tail = lax.slice_in_dim(cells, cells.shape[dim] - width, cells.shape[dim], axis=dim)
        cells = jnp.concatenate(
            [
                lax.ppermute(tail, axis, [(i, (i + 1) % count) for i in range(ends)]),
                cells,
                lax.ppermute(head, axis, [((i + 1) % count, i) for i in range(ends)]),
            ],
            axis=dim,
        )
    return cells


def partners(sizes):
    nx, ny, nz = sizes
    half = ny // 2
    gx, gy, gz = (lax.axis_index(name) for name in ("gx", "gy", "gz"))
    pair, core = lax.div(gy, 2), lax.rem(gy, 2)
    steps = [
        [(lax.rem(gz + d, nz), {"gz": lax.rem(gz + d, nz)}) for d in range(1, nz)],
        [(lax.rem(gx + d, nx), {"gx": lax.rem(gx + d, nx)}) for d in range(1, nx)],
        [
            (lax.rem(pair + d, half), {"gy": lax.rem(pair + d, half) * 2 + core})
            for d in range(1, half)
        ],
        [(1 - core, {"gy": pair * 2 + 1 - core})],
    ]
    return (gx, pair, core, gz), steps


def greet(devices):
    barrier = pltpu.get_barrier_semaphore()
    for device in devices:
        pl.semaphore_signal(barrier, inc=1, device_id=device, device_id_type=MESH)
    pl.semaphore_wait(barrier, len(devices))


class Sender:
    def __init__(self, send, recv):
        self.send, self.recv, self.used = send, recv, 0

    def start(self, src, dst, device):
        at = self.used
        self.used += 1
        copy = pltpu.make_async_remote_copy(
            src_ref=src,
            dst_ref=dst,
            send_sem=self.send.at[at],
            recv_sem=self.recv.at[at],
            device_id=device,
            device_id_type=MESH,
        )
        copy.start()
        return copy


def gather_kernel(sizes, x_ref, out_ref, send, recv):
    (gx, pair, core, gz), steps = partners(sizes)
    out_ref[gx, pair, core, gz] = x_ref[...]
    greet([device for step in steps for _, device in step])
    sender = Sender(send, recv)
    held = [
        out_ref.at[gx, pair, core, gz],
        out_ref.at[gx, pair, core],
        out_ref.at[:, pair, core],
        out_ref.at[:, :, core],
    ]
    for part, step in zip(held, steps):
        copies = [sender.start(part, part, device) for _, device in step]
        for copy in copies:
            copy.wait()


def count_partners(sizes):
    nx, ny, nz = sizes
    return (nz - 1) + (nx - 1) + (ny // 2 - 1) + 1


def gather(sizes, mine, rows):
    nx, ny, nz = sizes
    count = count_partners(sizes)
    return pl.pallas_call(
        functools.partial(gather_kernel, sizes),
        out_shape=jax.ShapeDtypeStruct((nx, ny // 2, 2, nz, rows, 128), mine.dtype),
        in_specs=[pl.BlockSpec(memory_space=pltpu.VMEM)],
        out_specs=pl.BlockSpec(memory_space=pltpu.VMEM),
        scratch_shapes=[pltpu.SemaphoreType.DMA((count,)), pltpu.SemaphoreType.DMA((count,))],
        compiler_params=pltpu.CompilerParams(
            collective_id=0, has_side_effects=True, vmem_limit_bytes=32 * 1024 * 1024
        ),
        name="gather_weights",
    )(mine)


def reduce_kernel(
    sizes, g_ref, own_ref, norm_ref, s0, r0, a0, s1, r1, a1, s2, r2, a2, s3, r3, ts, tr, send, recv
):
    nx, ny, nz = sizes
    half = ny // 2
    (gx, pair, core, gz), steps = partners(sizes)
    greet([device for step in steps for _, device in step])
    sender = Sender(send, recv)
    by_z, by_x, by_pair, by_core = steps

    s0[...] = g_ref[:, :, 1 - core].astype(jnp.bfloat16)
    sender.start(s0, r0, by_core[0][1]).wait()
    a0[...] = g_ref[:, :, core] + r0[...].astype(jnp.float32)

    def level(step, total, sbuf, rbuf, take, put):
        copies = []
        for at, (index, device) in enumerate(step):
            sbuf[at] = take(index).astype(jnp.bfloat16)
            copies.append(sender.start(sbuf.at[at], rbuf.at[at], device))
        for at, copy in enumerate(copies):
            copy.wait()
            total = total + rbuf[at].astype(jnp.float32)
        put[...] = total

    level(by_pair, a0[:, pair], s1, r1, lambda index: a0[:, index], a1)
    level(by_x, a1[gx], s2, r2, lambda index: a1[index], a2)
    level(by_z, a2[gz], s3, r3, lambda index: a2[index], own_ref)

    own = own_ref[...]
    tile = jnp.sum((own * own).reshape(own.shape[0] // 8, 8, 128), 0)
    at = 0
    for number, step in enumerate(steps):
        if not step:
            continue
        ts[number] = tile
        copies = []
        for _, device in step:
            copies.append((at, sender.start(ts.at[number], tr.at[at], device)))
            at += 1
        for slot, copy in copies:
            copy.wait()
            tile = tile + tr[slot]
    norm_ref[...] = tile


def reduce(sizes, gradient, rows):
    nx, ny, nz = sizes
    half = ny // 2
    count = count_partners(sizes)
    few = lambda n: max(n, 1)
    narrow, wide = jnp.bfloat16, jnp.float32
    vm = pltpu.VMEM
    return pl.pallas_call(
        functools.partial(reduce_kernel, sizes),
        out_shape=(
            jax.ShapeDtypeStruct((rows, 128), wide),
            jax.ShapeDtypeStruct((8, 128), wide),
        ),
        in_specs=[pl.BlockSpec(memory_space=pltpu.VMEM)],
        out_specs=(
            pl.BlockSpec(memory_space=pltpu.VMEM),
            pl.BlockSpec(memory_space=pltpu.VMEM),
        ),
        scratch_shapes=[
            vm((nx, half, nz, rows, 128), narrow),
            vm((nx, half, nz, rows, 128), narrow),
            vm((nx, half, nz, rows, 128), wide),
            vm((few(half - 1), nx, nz, rows, 128), narrow),
            vm((few(half - 1), nx, nz, rows, 128), narrow),
            vm((nx, nz, rows, 128), wide),
            vm((few(nx - 1), nz, rows, 128), narrow),
            vm((few(nx - 1), nz, rows, 128), narrow),
            vm((nz, rows, 128), wide),
            vm((few(nz - 1), rows, 128), narrow),
            vm((few(nz - 1), rows, 128), narrow),
            vm((4, 8, 128), wide),
            vm((count, 8, 128), wide),
            pltpu.SemaphoreType.DMA((2 * count,)),
            pltpu.SemaphoreType.DMA((2 * count,)),
        ],
        compiler_params=pltpu.CompilerParams(
            collective_id=1, has_side_effects=True, vmem_limit_bytes=48 * 1024 * 1024
        ),
        name="reduce_gradient",
    )(gradient)


def split_kernels(flat_weights):
    shapes = [(G, C + layer * G) for layer in range(4)] + [(C, C + 4 * G)]
    kernel_list = []
    offset = 0
    for outputs, inputs in shapes:
        length = 27 * outputs * inputs
        kernel_list.append(flat_weights[offset : offset + length].reshape(27, outputs, inputs))
        offset = offset + length
    return kernel_list


def channels_first(packed):
    return packed.reshape(packed.shape[0], packed.shape[1], -1, C).transpose(3, 0, 1, 2)


def grow_rim(values_in):
    return extended(values_in, (("gx", 1), ("gy", 2), ("gz", 3)), 1)


def signal_border(values_in):
    return extended(values_in, (("gx", 1), ("gy", 2), ("gz", 3)), 1)


def apply_kernel(padded, kernel, size_x, size_y, size_z):
    summed = None
    for offset_x in range(3):
        for offset_y in range(3):
            for offset_z in range(3):
                window = padded[
                    :,
                    offset_x : offset_x + size_x,
                    offset_y : offset_y + size_y,
                    offset_z : offset_z + size_z,
                ]
                window = window.reshape(padded.shape[0], -1)
                product = jnp.dot(
                    kernel[offset_x * 9 + offset_y * 3 + offset_z],
                    window,
                    preferred_element_type=jnp.float32,
                )
                summed = product if summed is None else summed + product
    return summed


def spread_back(padded, kernel, skipped, size_x, size_y, size_z):
    summed = None
    for offset_x in range(3):
        for offset_y in range(3):
            for offset_z in range(3):
                window = padded[
                    :,
                    2 - offset_x : 2 - offset_x + size_x,
                    2 - offset_y : 2 - offset_y + size_y,
                    2 - offset_z : 2 - offset_z + size_z,
                ]
                window = window.reshape(padded.shape[0], -1)
                product = lax.dot_general(
                    kernel[offset_x * 9 + offset_y * 3 + offset_z][:, skipped:],
                    window,
                    (((0,), (0,)), ((), ())),
                    preferred_element_type=jnp.float32,
                )
                summed = product if summed is None else summed + product
    return summed


def kernel_gradient(padded, signal, size_x, size_y, size_z):
    blocks = []
    for offset_x in range(3):
        for offset_y in range(3):
            for offset_z in range(3):
                window = padded[
                    :,
                    offset_x : offset_x + size_x,
                    offset_y : offset_y + size_y,
                    offset_z : offset_z + size_z,
                ]
                window = window.reshape(padded.shape[0], -1)
                blocks.append(
                    lax.dot_general(
                        signal, window, (((1,), (1,)), ((), ())), preferred_element_type=jnp.float32
                    )
                )
    return jnp.stack(blocks, 0)


def local(features, upstream, params, first_moment, second_moment):
    sizes = tuple(lax.axis_size(name) for name in ("gx", "gy", "gz"))
    share = params.shape[0]
    rows = -(-share // 2048) * 16
    spare = rows * 128 - share
    mine = jnp.pad(params.astype(jnp.bfloat16), (0, spare)).reshape(rows, 128)
    flat_weights = gather(sizes, mine, rows).reshape(-1, rows * 128)[:, :share].reshape(-1)
    kernel_list = split_kernels(flat_weights)
    field = channels_first(features)
    channels, size_x, size_y, size_z = field.shape
    signal_top = (RESIDUAL_SCALE * channels_first(upstream).astype(jnp.float32)).astype(
        jnp.bfloat16
    )
    paired = extended(jnp.concatenate([field, signal_top], 0), (("gx", 1), ("gy", 2), ("gz", 3)), 1)
    padded_input = paired[:channels]
    padded_top = paired[channels:]
    padded_pieces = [padded_input]
    stacked_list = []
    slopes = []
    for layer in range(4):
        stacked = jnp.concatenate(padded_pieces, 0)
        stacked_list.append(stacked)
        before = apply_kernel(stacked, kernel_list[layer], size_x, size_y, size_z)
        slope_now = jnp.where(before > 0, 1.0, LEAK_SLOPE)
        slopes.append(slope_now)
        growth = (before * slope_now).astype(jnp.bfloat16).reshape(-1, size_x, size_y, size_z)
        padded_pieces.append(grow_rim(growth))
    stacked = jnp.concatenate(padded_pieces, 0)
    stacked_list.append(stacked)
    last = apply_kernel(stacked, kernel_list[4], size_x, size_y, size_z)
    refined_first = (
        field.astype(jnp.float32) + RESIDUAL_SCALE * last.reshape(channels, size_x, size_y, size_z)
    ).astype(jnp.bfloat16)
    refined = refined_first.transpose(1, 2, 3, 0).reshape(features.shape)
    padded_signal = padded_top
    signals = [None] * 5
    signals[4] = signal_top.reshape(channels, -1)
    backward = [None] * 4
    for layer in range(4, 0, -1):
        if layer < 4:
            padded_signal = signal_border(signals[layer].reshape(-1, size_x, size_y, size_z))
        spread = spread_back(padded_signal, kernel_list[layer], channels, size_x, size_y, size_z)
        for target in range(layer):
            segment = spread[target * G : (target + 1) * G]
            backward[target] = segment if backward[target] is None else backward[target] + segment
        signals[layer - 1] = (backward[layer - 1] * slopes[layer - 1]).astype(jnp.bfloat16)
    grads = []
    for layer in range(5):
        grads.append(
            kernel_gradient(stacked_list[layer], signals[layer], size_x, size_y, size_z).reshape(-1)
        )
    gradient = jnp.concatenate(grads)
    padded = jnp.pad(gradient.reshape(-1, share), ((0, 0), (0, spare)))
    nx, ny, nz = sizes
    own_share, norm_tile = reduce(sizes, padded.reshape(nx, ny // 2, 2, nz, rows, 128), rows)
    own_share = own_share.reshape(-1)[:share]
    norm_sq = jnp.sum(norm_tile)
    factor = jnp.minimum(1.0, jnp.sqrt(flat_weights.shape[0] / (norm_sq + NORM_EPS)))
    clipped = own_share * factor
    new_first = BETA_ONE * first_moment + (1.0 - BETA_ONE) * clipped
    new_second = BETA_TWO * second_moment + (1.0 - BETA_TWO) * clipped * clipped
    first_hat = new_first / (1.0 - BETA_ONE**STEP)
    second_hat = new_second / (1.0 - BETA_TWO**STEP)
    new_params = params - LEARN_RATE * first_hat / (jnp.sqrt(second_hat) + ADAM_EPS)
    return (refined, new_params, new_first, new_second)


def solution(mesh):
    return jax.shard_map(
        local,
        mesh=mesh,
        in_specs=(
            P("gx", "gy", "gz"),
            P("gx", "gy", "gz"),
            P(("gx", "gy", "gz")),
            P(("gx", "gy", "gz")),
            P(("gx", "gy", "gz")),
        ),
        out_specs=(
            P("gx", "gy", "gz"),
            P(("gx", "gy", "gz")),
            P(("gx", "gy", "gz")),
            P(("gx", "gy", "gz")),
        ),
        check_vma=False,
    )
```

```python
import functools

import jax
import jax.numpy as jnp
from jax import lax
from jax.experimental import pallas as pl
from jax.experimental.pallas import tpu as pltpu
from jax.sharding import PartitionSpec as P

MESH = pl.DeviceIdType.MESH

C = 64
G = 32
STEP = 3


LEAK_SLOPE = 0.2
RESIDUAL_SCALE = 0.2
BETA_ONE = 0.9
BETA_TWO = 0.999
LEARN_RATE = 0.001
ADAM_EPS = 1e-08
NORM_EPS = 1e-06


def extended(cells, sides, width):
    for axis, dim in sides:
        count = lax.axis_size(axis)
        ends = count - 1
        head = lax.slice_in_dim(cells, 0, width, axis=dim)
        tail = lax.slice_in_dim(cells, cells.shape[dim] - width, cells.shape[dim], axis=dim)
        cells = jnp.concatenate(
            [
                lax.ppermute(tail, axis, [(i, (i + 1) % count) for i in range(ends)]),
                cells,
                lax.ppermute(head, axis, [((i + 1) % count, i) for i in range(ends)]),
            ],
            axis=dim,
        )
    return cells


def partners(sizes):
    nx, ny, nz = sizes
    half = ny // 2
    gx, gy, gz = (lax.axis_index(name) for name in ("gx", "gy", "gz"))
    pair, core = lax.div(gy, 2), lax.rem(gy, 2)
    steps = [
        [(lax.rem(gz + d, nz), {"gz": lax.rem(gz + d, nz)}) for d in range(1, nz)],
        [(lax.rem(gx + d, nx), {"gx": lax.rem(gx + d, nx)}) for d in range(1, nx)],
        [
            (lax.rem(pair + d, half), {"gy": lax.rem(pair + d, half) * 2 + core})
            for d in range(1, half)
        ],
        [(1 - core, {"gy": pair * 2 + 1 - core})],
    ]
    return (gx, pair, core, gz), steps


def greet(devices):
    barrier = pltpu.get_barrier_semaphore()
    for device in devices:
        pl.semaphore_signal(barrier, inc=1, device_id=device, device_id_type=MESH)
    pl.semaphore_wait(barrier, len(devices))


class Sender:
    def __init__(self, send, recv):
        self.send, self.recv, self.used = send, recv, 0

    def start(self, src, dst, device):
        at = self.used
        self.used += 1
        copy = pltpu.make_async_remote_copy(
            src_ref=src,
            dst_ref=dst,
            send_sem=self.send.at[at],
            recv_sem=self.recv.at[at],
            device_id=device,
            device_id_type=MESH,
        )
        copy.start()
        return copy


def gather_kernel(sizes, x_ref, out_ref, send, recv):
    (gx, pair, core, gz), steps = partners(sizes)
    out_ref[gx, pair, core, gz] = x_ref[...]
    greet([device for step in steps for _, device in step])
    sender = Sender(send, recv)
    held = [
        out_ref.at[gx, pair, core, gz],
        out_ref.at[gx, pair, core],
        out_ref.at[:, pair, core],
        out_ref.at[:, :, core],
    ]
    for part, step in zip(held, steps):
        copies = [sender.start(part, part, device) for _, device in step]
        for copy in copies:
            copy.wait()


def count_partners(sizes):
    nx, ny, nz = sizes
    return (nz - 1) + (nx - 1) + (ny // 2 - 1) + 1


def gather(sizes, mine, rows):
    nx, ny, nz = sizes
    count = count_partners(sizes)
    return pl.pallas_call(
        functools.partial(gather_kernel, sizes),
        out_shape=jax.ShapeDtypeStruct((nx, ny // 2, 2, nz, rows, 128), mine.dtype),
        in_specs=[pl.BlockSpec(memory_space=pltpu.VMEM)],
        out_specs=pl.BlockSpec(memory_space=pltpu.VMEM),
        scratch_shapes=[pltpu.SemaphoreType.DMA((count,)), pltpu.SemaphoreType.DMA((count,))],
        compiler_params=pltpu.CompilerParams(
            collective_id=0, has_side_effects=True, vmem_limit_bytes=32 * 1024 * 1024
        ),
        name="gather_weights",
    )(mine)


def reduce_kernel(
    sizes, g_ref, own_ref, norm_ref, s0, r0, a0, s1, r1, a1, s2, r2, a2, s3, r3, ts, tr, send, recv
):
    nx, ny, nz = sizes
    half = ny // 2
    (gx, pair, core, gz), steps = partners(sizes)
    greet([device for step in steps for _, device in step])
    sender = Sender(send, recv)
    by_z, by_x, by_pair, by_core = steps

    s0[...] = g_ref[:, :, 1 - core].astype(jnp.bfloat16)
    sender.start(s0, r0, by_core[0][1]).wait()
    a0[...] = g_ref[:, :, core] + r0[...].astype(jnp.float32)

    def level(step, total, sbuf, rbuf, take, put):
        copies = []
        for at, (index, device) in enumerate(step):
            sbuf[at] = take(index).astype(jnp.bfloat16)
            copies.append(sender.start(sbuf.at[at], rbuf.at[at], device))
        for at, copy in enumerate(copies):
            copy.wait()
            total = total + rbuf[at].astype(jnp.float32)
        put[...] = total

    level(by_pair, a0[:, pair], s1, r1, lambda index: a0[:, index], a1)
    level(by_x, a1[gx], s2, r2, lambda index: a1[index], a2)
    level(by_z, a2[gz], s3, r3, lambda index: a2[index], own_ref)

    own = own_ref[...]
    tile = jnp.sum((own * own).reshape(own.shape[0] // 8, 8, 128), 0)
    at = 0
    for number, step in enumerate(steps):
        if not step:
            continue
        ts[number] = tile
        copies = []
        for _, device in step:
            copies.append((at, sender.start(ts.at[number], tr.at[at], device)))
            at += 1
        for slot, copy in copies:
            copy.wait()
            tile = tile + tr[slot]
    norm_ref[...] = tile


def reduce(sizes, gradient, rows):
    nx, ny, nz = sizes
    half = ny // 2
    count = count_partners(sizes)
    few = lambda n: max(n, 1)
    narrow, wide = jnp.bfloat16, jnp.float32
    vm = pltpu.VMEM
    return pl.pallas_call(
        functools.partial(reduce_kernel, sizes),
        out_shape=(
            jax.ShapeDtypeStruct((rows, 128), wide),
            jax.ShapeDtypeStruct((8, 128), wide),
        ),
        in_specs=[pl.BlockSpec(memory_space=pltpu.VMEM)],
        out_specs=(
            pl.BlockSpec(memory_space=pltpu.VMEM),
            pl.BlockSpec(memory_space=pltpu.VMEM),
        ),
        scratch_shapes=[
            vm((nx, half, nz, rows, 128), narrow),
            vm((nx, half, nz, rows, 128), narrow),
            vm((nx, half, nz, rows, 128), wide),
            vm((few(half - 1), nx, nz, rows, 128), narrow),
            vm((few(half - 1), nx, nz, rows, 128), narrow),
            vm((nx, nz, rows, 128), wide),
            vm((few(nx - 1), nz, rows, 128), narrow),
            vm((few(nx - 1), nz, rows, 128), narrow),
            vm((nz, rows, 128), wide),
            vm((few(nz - 1), rows, 128), narrow),
            vm((few(nz - 1), rows, 128), narrow),
            vm((4, 8, 128), wide),
            vm((count, 8, 128), wide),
            pltpu.SemaphoreType.DMA((2 * count,)),
            pltpu.SemaphoreType.DMA((2 * count,)),
        ],
        compiler_params=pltpu.CompilerParams(
            collective_id=1, has_side_effects=True, vmem_limit_bytes=48 * 1024 * 1024
        ),
        name="reduce_gradient",
    )(gradient)


def split_kernels(flat_weights):
    shapes = [(G, C + layer * G) for layer in range(4)] + [(C, C + 4 * G)]
    kernel_list = []
    offset = 0
    for outputs, inputs in shapes:
        length = 27 * outputs * inputs
        kernel_list.append(flat_weights[offset : offset + length].reshape(27, outputs, inputs))
        offset = offset + length
    return kernel_list


def channels_last(packed):
    return packed.reshape(packed.shape[0], packed.shape[1], -1, C)


def grow_rim(values_in):
    return extended(values_in, (("gx", 0), ("gy", 1), ("gz", 2)), 1)


def correlate(padded, kernel, numbers):
    return lax.conv_general_dilated(
        padded[None],
        kernel.reshape((3, 3, 3) + kernel.shape[1:]),
        (1, 1, 1),
        "VALID",
        dimension_numbers=("NDHWC", numbers, "NDHWC"),
        preferred_element_type=jnp.float32,
    )[0]


def all_windows(padded, size_x, size_y, size_z):
    return jnp.stack(
        [
            padded[dx : dx + size_x, dy : dy + size_y, dz : dz + size_z].reshape(
                -1, padded.shape[3]
            )
            for dx in range(3)
            for dy in range(3)
            for dz in range(3)
        ],
        0,
    )


def local(features, upstream, params, first_moment, second_moment):
    sizes = tuple(lax.axis_size(name) for name in ("gx", "gy", "gz"))
    share = params.shape[0]
    rows = -(-share // 2048) * 16
    spare = rows * 128 - share
    mine = jnp.pad(params.astype(jnp.bfloat16), (0, spare)).reshape(rows, 128)
    flat_weights = gather(sizes, mine, rows).reshape(-1, rows * 128)[:, :share].reshape(-1)
    kernel_list = split_kernels(flat_weights)
    field = channels_last(features)
    size_x, size_y, size_z, channels = field.shape
    signal_top = (RESIDUAL_SCALE * channels_last(upstream).astype(jnp.float32)).astype(
        jnp.bfloat16
    )
    paired = grow_rim(jnp.concatenate([field, signal_top], 3))
    stacked = paired[..., :channels]
    padded_signal = paired[..., channels:]
    slopes = []
    for layer in range(4):
        before = correlate(stacked, kernel_list[layer], "DHWOI")
        slope_now = jnp.where(before > 0, 1.0, LEAK_SLOPE)
        slopes.append(slope_now)
        growth = (before * slope_now).astype(jnp.bfloat16)
        stacked = jnp.concatenate([stacked, grow_rim(growth)], 3)
    last = correlate(stacked, kernel_list[4], "DHWOI")
    refined = (
        (field.astype(jnp.float32) + RESIDUAL_SCALE * last)
        .astype(jnp.bfloat16)
        .reshape(features.shape)
    )
    signals = [None] * 5
    signals[4] = signal_top
    backward = [None] * 4
    for layer in range(4, 0, -1):
        if layer < 4:
            padded_signal = grow_rim(signals[layer])
        spread = correlate(padded_signal, kernel_list[layer][::-1, :, channels:], "DHWIO")
        for target in range(layer):
            segment = spread[..., target * G : (target + 1) * G]
            backward[target] = segment if backward[target] is None else backward[target] + segment
        signals[layer - 1] = (backward[layer - 1] * slopes[layer - 1]).astype(jnp.bfloat16)
    windows = all_windows(stacked, size_x, size_y, size_z)
    joined = jnp.concatenate(signals, 3).reshape(-1, 4 * G + channels)
    products = lax.dot_general(
        joined, windows, (((0,), (1,)), ((), ())), preferred_element_type=jnp.float32
    )
    grads = []
    for layer in range(5):
        outputs = G if layer < 4 else channels
        block = products[layer * G : layer * G + outputs, :, : channels + layer * G]
        grads.append(block.transpose(1, 0, 2).reshape(-1))
    gradient = jnp.concatenate(grads)
    padded = jnp.pad(gradient.reshape(-1, share), ((0, 0), (0, spare)))
    nx, ny, nz = sizes
    own_share, norm_tile = reduce(sizes, padded.reshape(nx, ny // 2, 2, nz, rows, 128), rows)
    own_share = own_share.reshape(-1)[:share]
    norm_sq = jnp.sum(norm_tile)
    factor = jnp.minimum(1.0, jnp.sqrt(flat_weights.shape[0] / (norm_sq + NORM_EPS)))
    clipped = own_share * factor
    new_first = BETA_ONE * first_moment + (1.0 - BETA_ONE) * clipped
    new_second = BETA_TWO * second_moment + (1.0 - BETA_TWO) * clipped * clipped
    first_hat = new_first / (1.0 - BETA_ONE**STEP)
    second_hat = new_second / (1.0 - BETA_TWO**STEP)
    new_params = params - LEARN_RATE * first_hat / (jnp.sqrt(second_hat) + ADAM_EPS)
    return (refined, new_params, new_first, new_second)


def solution(mesh):
    return jax.shard_map(
        local,
        mesh=mesh,
        in_specs=(
            P("gx", "gy", "gz"),
            P("gx", "gy", "gz"),
            P(("gx", "gy", "gz")),
            P(("gx", "gy", "gz")),
            P(("gx", "gy", "gz")),
        ),
        out_specs=(
            P("gx", "gy", "gz"),
            P(("gx", "gy", "gz")),
            P(("gx", "gy", "gz")),
            P(("gx", "gy", "gz")),
        ),
        check_vma=False,
    )
```

```python
import functools

import jax
import jax.numpy as jnp
from jax import lax
from jax.experimental import pallas as pl
from jax.experimental.pallas import tpu as pltpu
from jax.sharding import PartitionSpec as P

MESH = pl.DeviceIdType.MESH

C = 64
G = 32
STEP = 3


LEAK_SLOPE = 0.2
RESIDUAL_SCALE = 0.2
BETA_ONE = 0.9
BETA_TWO = 0.999
LEARN_RATE = 0.001
ADAM_EPS = 1e-08
NORM_EPS = 1e-06


def partners(sizes):
    nx, ny, nz = sizes
    half = ny // 2
    gx, gy, gz = (lax.axis_index(name) for name in ("gx", "gy", "gz"))
    pair, core = lax.div(gy, 2), lax.rem(gy, 2)
    steps = [
        [(lax.rem(gz + d, nz), {"gz": lax.rem(gz + d, nz)}) for d in range(1, nz)],
        [(lax.rem(gx + d, nx), {"gx": lax.rem(gx + d, nx)}) for d in range(1, nx)],
        [
            (lax.rem(pair + d, half), {"gy": lax.rem(pair + d, half) * 2 + core})
            for d in range(1, half)
        ],
        [(1 - core, {"gy": pair * 2 + 1 - core})],
    ]
    return (gx, pair, core, gz), steps


def greet(devices):
    barrier = pltpu.get_barrier_semaphore()
    for device in devices:
        pl.semaphore_signal(barrier, inc=1, device_id=device, device_id_type=MESH)
    pl.semaphore_wait(barrier, len(devices))


class Sender:
    def __init__(self, send, recv):
        self.send, self.recv, self.used = send, recv, 0

    def start(self, src, dst, device):
        at = self.used
        self.used += 1
        copy = pltpu.make_async_remote_copy(
            src_ref=src,
            dst_ref=dst,
            send_sem=self.send.at[at],
            recv_sem=self.recv.at[at],
            device_id=device,
            device_id_type=MESH,
        )
        copy.start()
        return copy


def gather_kernel(sizes, x_ref, out_ref, send, recv):
    (gx, pair, core, gz), steps = partners(sizes)
    out_ref[gx, pair, core, gz] = x_ref[...]
    greet([device for step in steps for _, device in step])
    sender = Sender(send, recv)
    held = [
        out_ref.at[gx, pair, core, gz],
        out_ref.at[gx, pair, core],
        out_ref.at[:, pair, core],
        out_ref.at[:, :, core],
    ]
    for part, step in zip(held, steps):
        copies = [sender.start(part, part, device) for _, device in step]
        for copy in copies:
            copy.wait()


def count_partners(sizes):
    nx, ny, nz = sizes
    return (nz - 1) + (nx - 1) + (ny // 2 - 1) + 1


def gather(sizes, mine, rows):
    nx, ny, nz = sizes
    count = count_partners(sizes)
    return pl.pallas_call(
        functools.partial(gather_kernel, sizes),
        out_shape=jax.ShapeDtypeStruct((nx, ny // 2, 2, nz, rows, 128), mine.dtype),
        in_specs=[pl.BlockSpec(memory_space=pltpu.VMEM)],
        out_specs=pl.BlockSpec(memory_space=pltpu.VMEM),
        scratch_shapes=[pltpu.SemaphoreType.DMA((count,)), pltpu.SemaphoreType.DMA((count,))],
        compiler_params=pltpu.CompilerParams(
            collective_id=0, has_side_effects=True, vmem_limit_bytes=32 * 1024 * 1024
        ),
        name="gather_weights",
    )(mine)


def reduce_kernel(
    sizes, g_ref, own_ref, norm_ref, s0, r0, a0, s1, r1, a1, s2, r2, a2, s3, r3, ts, tr, send, recv
):
    nx, ny, nz = sizes
    half = ny // 2
    (gx, pair, core, gz), steps = partners(sizes)
    greet([device for step in steps for _, device in step])
    sender = Sender(send, recv)
    by_z, by_x, by_pair, by_core = steps

    s0[...] = g_ref[:, :, 1 - core].astype(jnp.bfloat16)
    sender.start(s0, r0, by_core[0][1]).wait()
    a0[...] = g_ref[:, :, core] + r0[...].astype(jnp.float32)

    def level(step, total, sbuf, rbuf, take, put):
        copies = []
        for at, (index, device) in enumerate(step):
            sbuf[at] = take(index).astype(jnp.bfloat16)
            copies.append(sender.start(sbuf.at[at], rbuf.at[at], device))
        for at, copy in enumerate(copies):
            copy.wait()
            total = total + rbuf[at].astype(jnp.float32)
        put[...] = total

    level(by_pair, a0[:, pair], s1, r1, lambda index: a0[:, index], a1)
    level(by_x, a1[gx], s2, r2, lambda index: a1[index], a2)
    level(by_z, a2[gz], s3, r3, lambda index: a2[index], own_ref)

    own = own_ref[...]
    tile = jnp.sum((own * own).reshape(own.shape[0] // 8, 8, 128), 0)
    at = 0
    for number, step in enumerate(steps):
        if not step:
            continue
        ts[number] = tile
        copies = []
        for _, device in step:
            copies.append((at, sender.start(ts.at[number], tr.at[at], device)))
            at += 1
        for slot, copy in copies:
            copy.wait()
            tile = tile + tr[slot]
    norm_ref[...] = tile


def reduce(sizes, gradient, rows):
    nx, ny, nz = sizes
    half = ny // 2
    count = count_partners(sizes)
    few = lambda n: max(n, 1)
    narrow, wide = jnp.bfloat16, jnp.float32
    vm = pltpu.VMEM
    return pl.pallas_call(
        functools.partial(reduce_kernel, sizes),
        out_shape=(
            jax.ShapeDtypeStruct((rows, 128), wide),
            jax.ShapeDtypeStruct((8, 128), wide),
        ),
        in_specs=[pl.BlockSpec(memory_space=pltpu.VMEM)],
        out_specs=(
            pl.BlockSpec(memory_space=pltpu.VMEM),
            pl.BlockSpec(memory_space=pltpu.VMEM),
        ),
        scratch_shapes=[
            vm((nx, half, nz, rows, 128), narrow),
            vm((nx, half, nz, rows, 128), narrow),
            vm((nx, half, nz, rows, 128), wide),
            vm((few(half - 1), nx, nz, rows, 128), narrow),
            vm((few(half - 1), nx, nz, rows, 128), narrow),
            vm((nx, nz, rows, 128), wide),
            vm((few(nx - 1), nz, rows, 128), narrow),
            vm((few(nx - 1), nz, rows, 128), narrow),
            vm((nz, rows, 128), wide),
            vm((few(nz - 1), rows, 128), narrow),
            vm((few(nz - 1), rows, 128), narrow),
            vm((4, 8, 128), wide),
            vm((count, 8, 128), wide),
            pltpu.SemaphoreType.DMA((2 * count,)),
            pltpu.SemaphoreType.DMA((2 * count,)),
        ],
        compiler_params=pltpu.CompilerParams(
            collective_id=1, has_side_effects=True, vmem_limit_bytes=48 * 1024 * 1024
        ),
        name="reduce_gradient",
    )(gradient)


def split_kernels(flat_weights):
    shapes = [(G, C + layer * G) for layer in range(4)] + [(C, C + 4 * G)]
    kernel_list = []
    offset = 0
    for outputs, inputs in shapes:
        length = 27 * outputs * inputs
        kernel_list.append(flat_weights[offset : offset + length].reshape(27, outputs, inputs))
        offset = offset + length
    return kernel_list


def channels_last(packed):
    return packed.reshape(packed.shape[0], packed.shape[1], -1, C)


def rim_kernel(sizes, u_ref, wide_ref, zr, xr, ys, yr, zs, send, recv):
    size_x, size_y = u_ref.shape[0], u_ref.shape[1]
    names = ("gx", "gy", "gz")
    places = [lax.axis_index(name) for name in names]

    def sides(axis):
        me, name = places[axis], names[axis]
        return (me > 0, {name: me - 1}), (me < sizes[axis] - 1, {name: me + 1})

    xr[...] = jnp.zeros_like(xr)
    yr[...] = jnp.zeros_like(yr)
    zr[...] = jnp.zeros_like(zr)
    barrier = pltpu.get_barrier_semaphore()
    for axis in range(3):
        for there, device in sides(axis):

            @pl.when(there)
            def _(device=device):
                pl.semaphore_signal(barrier, inc=1, device_id=device, device_id_type=MESH)

    peers = 0
    for me, size in zip(places, sizes):
        peers = peers + lax.div(me + size - 1, size) + lax.div(2 * size - 2 - me, size)
    pl.semaphore_wait(barrier, peers)

    def swap(axis, sources, landing):
        pair = sides(axis)
        copies = []
        for way in range(2):
            there, device = pair[way]
            copy = pltpu.make_async_remote_copy(
                src_ref=sources[way],
                dst_ref=landing.at[1 - way],
                send_sem=send.at[2 * axis + way],
                recv_sem=recv.at[2 * axis + way],
                device_id=device,
                device_id_type=MESH,
            )
            copies.append(copy)

            @pl.when(there)
            def _(copy=copy):
                copy.start()

        for way in range(2):

            @pl.when(pair[way][0])
            def _(copy=copies[way]):
                copy.wait_send()

            @pl.when(pair[1 - way][0])
            def _(copy=copies[way]):
                copy.wait_recv()

    wide_ref[1 : size_x + 1, 1 : size_y + 1] = u_ref[...]
    swap(0, (u_ref.at[0], u_ref.at[size_x - 1]), xr)
    wide_ref[0, 1 : size_y + 1] = xr[0]
    wide_ref[size_x + 1, 1 : size_y + 1] = xr[1]
    ys[0] = wide_ref[:, 1]
    ys[1] = wide_ref[:, size_y]
    swap(1, (ys.at[0], ys.at[1]), yr)
    wide_ref[:, 0] = yr[0]
    wide_ref[:, size_y + 1] = yr[1]
    zs[0] = wide_ref[:, :, 0, :]
    zs[1] = wide_ref[:, :, wide_ref.shape[2] - 1, :]
    swap(2, (zs.at[0], zs.at[1]), zr)


def grow_rim(values_in, number):
    sizes = tuple(lax.axis_size(name) for name in ("gx", "gy", "gz"))
    size_x, size_y, size_z, channels = values_in.shape
    kind = jnp.float32
    vm = pltpu.VMEM
    wide, ends = pl.pallas_call(
        functools.partial(rim_kernel, sizes),
        out_shape=(
            jax.ShapeDtypeStruct((size_x + 2, size_y + 2, size_z, channels), kind),
            jax.ShapeDtypeStruct((2, size_x + 2, size_y + 2, channels), kind),
        ),
        in_specs=[pl.BlockSpec(memory_space=pltpu.VMEM)],
        out_specs=(
            pl.BlockSpec(memory_space=pltpu.VMEM),
            pl.BlockSpec(memory_space=pltpu.VMEM),
        ),
        scratch_shapes=[
            vm((2, size_y, size_z, channels), kind),
            vm((2, size_x + 2, size_z, channels), kind),
            vm((2, size_x + 2, size_z, channels), kind),
            vm((2, size_x + 2, size_y + 2, channels), kind),
            pltpu.SemaphoreType.DMA((6,)),
            pltpu.SemaphoreType.DMA((6,)),
        ],
        compiler_params=pltpu.CompilerParams(
            collective_id=number, has_side_effects=True, vmem_limit_bytes=32 * 1024 * 1024
        ),
        name="rim_exchange",
    )(values_in.astype(kind))
    return jnp.concatenate(
        [ends[0][:, :, None], wide, ends[1][:, :, None]], 2
    ).astype(jnp.bfloat16)


def correlate(padded, kernel, numbers):
    return lax.conv_general_dilated(
        padded[None],
        kernel.reshape((3, 3, 3) + kernel.shape[1:]),
        (1, 1, 1),
        "VALID",
        dimension_numbers=("NDHWC", numbers, "NDHWC"),
        preferred_element_type=jnp.float32,
    )[0]


def all_windows(padded, size_x, size_y, size_z):
    return jnp.stack(
        [
            padded[dx : dx + size_x, dy : dy + size_y, dz : dz + size_z].reshape(
                -1, padded.shape[3]
            )
            for dx in range(3)
            for dy in range(3)
            for dz in range(3)
        ],
        0,
    )


def local(features, upstream, params, first_moment, second_moment):
    sizes = tuple(lax.axis_size(name) for name in ("gx", "gy", "gz"))
    share = params.shape[0]
    rows = -(-share // 2048) * 16
    spare = rows * 128 - share
    mine = jnp.pad(params.astype(jnp.bfloat16), (0, spare)).reshape(rows, 128)
    flat_weights = gather(sizes, mine, rows).reshape(-1, rows * 128)[:, :share].reshape(-1)
    kernel_list = split_kernels(flat_weights)
    field = channels_last(features)
    size_x, size_y, size_z, channels = field.shape
    signal_top = (RESIDUAL_SCALE * channels_last(upstream).astype(jnp.float32)).astype(
        jnp.bfloat16
    )
    paired = grow_rim(jnp.concatenate([field, signal_top], 3), 2)
    stacked = paired[..., :channels]
    padded_signal = paired[..., channels:]
    slopes = []
    for layer in range(4):
        before = correlate(stacked, kernel_list[layer], "DHWOI")
        slope_now = jnp.where(before > 0, 1.0, LEAK_SLOPE)
        slopes.append(slope_now)
        growth = (before * slope_now).astype(jnp.bfloat16)
        stacked = jnp.concatenate([stacked, grow_rim(growth, 3)], 3)
    last = correlate(stacked, kernel_list[4], "DHWOI")
    refined = (
        (field.astype(jnp.float32) + RESIDUAL_SCALE * last)
        .astype(jnp.bfloat16)
        .reshape(features.shape)
    )
    signals = [None] * 5
    signals[4] = signal_top
    backward = [None] * 4
    for layer in range(4, 0, -1):
        if layer < 4:
            padded_signal = grow_rim(signals[layer], 3)
        spread = correlate(padded_signal, kernel_list[layer][::-1, :, channels:], "DHWIO")
        for target in range(layer):
            segment = spread[..., target * G : (target + 1) * G]
            backward[target] = segment if backward[target] is None else backward[target] + segment
        signals[layer - 1] = (backward[layer - 1] * slopes[layer - 1]).astype(jnp.bfloat16)
    windows = all_windows(stacked, size_x, size_y, size_z)
    joined = jnp.concatenate(signals, 3).reshape(-1, 4 * G + channels)
    products = lax.dot_general(
        joined, windows, (((0,), (1,)), ((), ())), preferred_element_type=jnp.float32
    )
    grads = []
    for layer in range(5):
        outputs = G if layer < 4 else channels
        block = products[layer * G : layer * G + outputs, :, : channels + layer * G]
        grads.append(block.transpose(1, 0, 2).reshape(-1))
    gradient = jnp.concatenate(grads)
    padded = jnp.pad(gradient.reshape(-1, share), ((0, 0), (0, spare)))
    nx, ny, nz = sizes
    own_share, norm_tile = reduce(sizes, padded.reshape(nx, ny // 2, 2, nz, rows, 128), rows)
    own_share = own_share.reshape(-1)[:share]
    norm_sq = jnp.sum(norm_tile)
    factor = jnp.minimum(1.0, jnp.sqrt(flat_weights.shape[0] / (norm_sq + NORM_EPS)))
    clipped = own_share * factor
    new_first = BETA_ONE * first_moment + (1.0 - BETA_ONE) * clipped
    new_second = BETA_TWO * second_moment + (1.0 - BETA_TWO) * clipped * clipped
    first_hat = new_first / (1.0 - BETA_ONE**STEP)
    second_hat = new_second / (1.0 - BETA_TWO**STEP)
    new_params = params - LEARN_RATE * first_hat / (jnp.sqrt(second_hat) + ADAM_EPS)
    return (refined, new_params, new_first, new_second)


def solution(mesh):
    return jax.shard_map(
        local,
        mesh=mesh,
        in_specs=(
            P("gx", "gy", "gz"),
            P("gx", "gy", "gz"),
            P(("gx", "gy", "gz")),
            P(("gx", "gy", "gz")),
            P(("gx", "gy", "gz")),
        ),
        out_specs=(
            P("gx", "gy", "gz"),
            P(("gx", "gy", "gz")),
            P(("gx", "gy", "gz")),
            P(("gx", "gy", "gz")),
        ),
        check_vma=False,
    )
```
